32 devices in a mesh: grp: 2 (over x), row: 8 (over z, y), col: 2 (over core).
Axes of the slice: x: 2, y: 2, z: 4, core: 2. Of those that a mesh axis runs over, the one named last changes fastest.
Arguments:
- geometry: bfloat16 [32, 7, 1024], P(('grp', 'row'), None, 'col'), parts along dimension 0, may hold values from -0.5 to 4, as said below
- currents: bfloat16 [32, 64, 1024], P(('grp', 'row'), None, 'col'), parts along dimension 0, may hold values from -6 to 6
- pair_count: int32 [32], P('grp'), parts along dimension 0, may hold values from 1 to 36, 192 in all
- pair_target: int32 [384], P('grp'), parts along dimension 0, may hold values from 0 to 15
Outputs:
- voltage: float32 [32, 64, 1024], P(('grp', 'row'), None, 'col'), parts along dimension 0
The draws below stay inside these ranges and needn't reach their ends.
There are 2 independent parts, one for each index of `grp`. The reference program is written for one: setup_inputs(seed, part) draws one part's arguments, and reference() takes and returns one part's arrays. A program takes and returns all parts, laid end to end along the dimension named above; each array names one. Nothing has to cross between parts.
Inputs may be any that keep to these rules, and one draw needn't show every extreme that they name: `pair_count`: each cluster lists 1 to 36 pairs, 192 in all, and some cluster exactly 36. `geometry`: component 6 (radius) lies in 0.1 to 0.4; positions lie in 0 to 4.
All inputs are finite; a program needn't handle non-finite values.
Results may differ from the reference program's by a relative error of at most 0.0029.
Values may be sent and summed in bfloat16 or wider, within the bound.
No kernel may reach another device: no remote copies, remote signals or barrier semaphores. Data moves between devices by JAX's collectives and lax.ppermute only.
A program may use at most 128 MiB of HBM per device.

```python
import math
import jax
import jax.numpy as jnp
import numpy as np
from jax import lax

CELLS_C = 1024
COLS = 64
CLUSTERS = 16
PAIRS = 192
MOSTP = 36


def draw_geometry(key, part):
    key = jax.random.fold_in(key, 11)
    key_pos, key_tan, key_rad = jax.random.split(key, 3)
    positions = jax.random.uniform(key_pos, (CLUSTERS, 3, CELLS_C), jnp.float32, 0.0, 4.0)
    tangents = jnp.clip(0.07 * jax.random.normal(key_tan, (CLUSTERS, 3, CELLS_C), jnp.float32), -0.4, 0.4)
    radius = jnp.exp(jax.random.uniform(key_rad, (CLUSTERS, 1, CELLS_C), jnp.float32, math.log(0.1), math.log(0.4)))
    return jnp.concatenate([positions, tangents, radius], axis=1).astype(jnp.bfloat16)


def set_ends(array, rng, low, largest):
    shape = array.shape
    index_at = [jax.random.randint(jax.random.fold_in(rng, axis), (), 0, shape[axis]) for axis in range(len(shape))]
    array = array.at[tuple(index_at)].set(low)
    longest = shape.index(max(shape))
    index_at[longest] = (index_at[longest] + 1) % shape[longest]
    return array.at[tuple(index_at)].set(largest)


def levels(key, dims, cuts, least, high):
    def one(axis_at, shards_of):
        steps = jax.random.uniform(jax.random.fold_in(jax.random.fold_in(key, 6), axis_at), (shards_of,), jnp.float32, least / len(cuts), high / len(cuts))
        return jnp.repeat(jnp.exp(steps), dims[axis_at] // shards_of).reshape((-1,) + (1,) * (len(dims) - axis_at - 1))

    factor_of = one(*cuts[0])
    for cut in cuts[1:]:
        factor_of = factor_of * one(*cut)
    return factor_of


def length_profile(number_of, total, limit, lean):
    weights = [(1 << 20) // math.isqrt(grade ** lean) + 1 for grade in range(2, number_of + 1)]
    surplus, counts = total - limit - (number_of - 1), [1] * (number_of - 1)
    while surplus > 0:
        candidates = [i for i in range(number_of - 1) if counts[i] < limit]
        pool, remaining = sum([weights[i] for i in candidates]), surplus
        for i in candidates:
            extra = min(limit - counts[i], max(1, remaining * weights[i] // pool), surplus)
            counts[i] = counts[i] + extra
            surplus = surplus - extra
    return np.array([limit] + counts)


def uneven(own_key, amount, total, reach, lean):
    if amount == 2:
        one = jax.random.randint(own_key, (), max(1, total - reach), min(reach, total - 1) + 1)
        return jnp.stack([one, total - one])
    sizes = jnp.asarray(length_profile(amount, total, reach, lean), jnp.int32)
    pairs = (amount - 1) // 2
    giver, taker = sizes[1:1 + 2 * pairs:2], sizes[2:2 + 2 * pairs:2]
    slack = jnp.minimum(giver - 1, reach - taker)
    shifted = jax.random.randint(jax.random.fold_in(own_key, 1), (pairs,), 0, 1 << 20) % (slack + 1)
    sizes = sizes.at[1:1 + 2 * pairs:2].set(giver - shifted).at[2:2 + 2 * pairs:2].set(taker + shifted)
    return sizes[jax.random.permutation(jax.random.fold_in(own_key, 2), amount)]


def scatter_about(key, shape, scale, limit, cuts=(), held_as=jnp.bfloat16):
    result = scale * jax.random.normal(key, shape, jnp.float32)
    if cuts:
        result = result * levels(key, shape, cuts, -0.22, 0.18)
    return jnp.clip(result, -limit, limit).astype(held_as)


def setup_inputs(seed: int = 0, part: int = 0) -> dict:
    streams_of = jax.random.split(jax.random.key(seed), 5)
    part_splits = jax.random.split(jax.random.fold_in(streams_of[4], part), 5)
    geometry = draw_geometry(jax.random.fold_in(jax.random.fold_in(streams_of[4], part), 71), part)
    currents = scatter_about(part_splits[1], (CLUSTERS, COLS, CELLS_C), 1.0, 6.0, ((0, 8), (2, 2)))
    pair_count = uneven(part_splits[2], CLUSTERS, PAIRS, MOSTP, 2).astype(jnp.int32)
    pair_target = set_ends(jax.random.randint(part_splits[3], (PAIRS,), 0, CLUSTERS), jax.random.fold_in(part_splits[3], 1), 0, CLUSTERS - 1).astype(jnp.int32)
    return {"geometry": geometry, "currents": currents, "pair_count": pair_count, "pair_target": pair_target}


def pair_block(row_geometry, col_geometry):
    distance_sq = row_geometry[6][:, None] * row_geometry[6][:, None] + col_geometry[6][None, :] * col_geometry[6][None, :]
    coupling = jnp.zeros_like(distance_sq)
    for comp in range(3):
        spread = row_geometry[comp][:, None] - col_geometry[comp][None, :]
        distance_sq = distance_sq + spread * spread
        coupling = coupling + row_geometry[comp + 3][:, None] * col_geometry[comp + 3][None, :]
    return (coupling * lax.rsqrt(distance_sq)).astype(jnp.bfloat16)

def reference(geometry, currents, pair_count, pair_target):
    geometry_all = geometry.astype(jnp.float32)
    count_ends = jnp.cumsum(pair_count).astype(jnp.int32)
    totals = jnp.zeros((CLUSTERS, COLS, CELLS_C), jnp.float32)

    def step(totals, index):
        first = jnp.sum((count_ends <= index).astype(jnp.int32)).astype(jnp.int32)
        second = pair_target[index].astype(jnp.int32)
        kernel_tile = pair_block(geometry_all[first], geometry_all[second])
        forward = jnp.dot(currents[second], kernel_tile.T, preferred_element_type=jnp.float32)
        backward = jnp.dot(currents[first], kernel_tile, preferred_element_type=jnp.float32)
        totals = totals.at[first].add(forward)
        totals = totals.at[second].add(backward)
        return (totals, None)
    totals, unused = lax.scan(step, totals, jnp.arange(PAIRS, dtype=jnp.int32))
    return totals
```

```python
import jax
import jax.numpy as jnp
import numpy as np
from jax import lax
from jax.experimental import pallas as pl
from jax.experimental.pallas import tpu as pltpu
from jax.sharding import PartitionSpec as P

F32 = jnp.float32
BF16 = jnp.bfloat16
NN = (((1,), (0,)), ((), ()))
NT = (((1,), (1,)), ((), ()))
COLS = 64
PACK = 80
VM = pl.BlockSpec(memory_space=pltpu.VMEM)
SM = pl.BlockSpec(memory_space=pltpu.SMEM)
PARAMS = pltpu.CompilerParams(vmem_limit_bytes=44 * 2**20)


def pack_kernel(geometry, currents, packet, block):
    for c in range(geometry.shape[0]):
        g = geometry[c].astype(F32)
        s = g[0:1] * g[0:1] + g[1:2] * g[1:2] + g[2:3] * g[2:3] + g[6:7] * g[6:7]
        s0 = s.astype(BF16).astype(F32)
        s1 = (s - s0).astype(BF16).astype(F32)
        s2 = s - s0 - s1
        one = jnp.ones_like(s)
        rows = jnp.concatenate([g[0:3], one, one, one, s0, s1, s2, g[3:6], jnp.zeros((4, s.shape[1]), F32)], 0)
        rows = rows.astype(BF16)
        packet[c, 0:COLS] = currents[c]
        packet[c, COLS:PACK] = rows
        block[c] = rows


def tiles(sources, weights, offset, left, tangents, acc, d0, d1, k0, k1):
    dist, kern = (d0, d1), (k0, k1)
    nc = left.shape[0]
    for j, source in enumerate(sources):
        nd = source.shape[0]

        def one(d, carry, source=source, base=offset + sum(s.shape[0] for s in sources[:j])):
            rows = source[d, COLS:PACK]
            along = rows.astype(F32)
            for c in range(nc):
                dist[c][...] = lax.dot_general(left[c], rows, NN, preferred_element_type=F32)
            for c in range(nc):
                spread = rows.shape[1] // 128
                coupling = 0.0
                for k in range(3):
                    coupling = coupling + jnp.concatenate([tangents[c, k]] * spread, 1) * along[9 + k : 10 + k]
                kern[c][...] = (coupling * lax.rsqrt(dist[c][...])).astype(BF16)
            for c in range(nc):
                part = lax.dot_general(kern[c][...], source[d, 0:COLS], NT, preferred_element_type=F32)
                acc[c] += weights[c, base + d] * part
            return carry

        lax.fori_loop(0, nd, one, 0)


def first_kernel(packet, other, weights, acc, left, tangents, d0, d1, k0, k1):
    half = other.shape[2]
    for c in range(left.shape[0]):
        for h, rows in enumerate((packet[c, COLS:PACK], other[c])):
            g = rows.astype(F32)
            cells = slice(h * half, (h + 1) * half)
            side = jnp.concatenate([-2.0 * g[0:3], g[6:9], g[3:6], jnp.zeros((7, half), F32)], 0)
            left[c, cells] = side.T.astype(BF16)
            across = jnp.concatenate([g[9:12], jnp.zeros((5, half), F32)], 0).T
            for k in range(3):
                tangents[c, k, cells] = jnp.broadcast_to(across[:, k : k + 1], (half, 128))
    acc[...] = jnp.zeros_like(acc)
    tiles((packet,), weights, 0, left, tangents, acc, d0, d1, k0, k1)


def step_kernel(offset, up, down, weights, left, tangents, acc_in, acc, d0, d1, k0, k1):
    acc[...] = acc_in[...]
    tiles((up, down), weights, offset, left, tangents, acc, d0, d1, k0, k1)


def last_kernel(offset, up, down, weights, left, tangents, acc_in, keep, send, acc, d0, d1, k0, k1):
    acc[...] = acc_in[...]
    tiles((up, down), weights, offset, left, tangents, acc, d0, d1, k0, k1)
    half = keep.shape[2]
    for c in range(keep.shape[0]):
        keep[c] = acc[c, 0:half].T
        send[c] = acc[c, half:].T


def ring_of(n):
    if n == 8:
        return [0, 2, 4, 6, 7, 5, 3, 1]
    return list(range(n))


def body(geometry, currents, pair_count, pair_target):
    nc, _, half = geometry.shape
    n = lax.axis_size("row")
    clusters = pair_count.shape[0]
    shape = jax.ShapeDtypeStruct
    packet, block = pl.pallas_call(
        pack_kernel,
        out_shape=(shape((nc, PACK, half), BF16), shape((nc, 16, half), BF16)),
        in_specs=[VM, VM],
        out_specs=(VM, VM),
    )(geometry, currents)
    other = lax.ppermute(block, "col", [(0, 1), (1, 0)])

    ring = ring_of(n)
    forward = [(ring[i], ring[(i + 1) % n]) for i in range(n)]
    backward = [(b, a) for a, b in forward]
    steps = n // 2
    place = np.argsort(ring)
    order = np.zeros((n, n * nc), np.int32)
    for r in range(n):
        at = [r * nc + i for i in range(nc)]
        for s in range(1, steps + 1):
            before, after = ring[(place[r] - s) % n], ring[(place[r] + s) % n]
            if s < steps:
                at += [before * nc + i for i in range(nc)] + [after * nc + i for i in range(nc)]
            else:
                at += [before * nc + i for i in range(nc)]
        order[r] = at
    row = lax.axis_index("row")
    second = lax.dynamic_slice_in_dim(jnp.asarray(order), row, 1, 0)[0]
    own = row * nc + jnp.arange(nc)
    ends = jnp.sum(jnp.where(np.tri(clusters, dtype=bool), pair_count[None, :], 0), 1)
    first_of = jnp.sum((ends[:, None] <= jnp.arange(pair_target.shape[0])[None, :]).astype(jnp.int32), 0)
    is_a = (first_of[None, None, :] == own[:, None, None]) & (pair_target[None, None, :] == second[None, :, None])
    is_b = (first_of[None, None, :] == second[None, :, None]) & (pair_target[None, None, :] == own[:, None, None])
    weights = jnp.sum(is_a.astype(F32) + is_b.astype(F32), 2)

    cells = 2 * half

    def cost(nd):
        count = nc * nd * cells * half
        return pl.CostEstimate(flops=600 * count, bytes_accessed=1 << 20, transcendentals=count)

    scratch = [pltpu.VMEM((cells, half), F32)] * 2 + [pltpu.VMEM((cells, half), BF16)] * 2
    acc_shape = shape((nc, cells, COLS), F32)
    acc, left, tangents = pl.pallas_call(
        first_kernel,
        out_shape=(acc_shape, shape((nc, cells, 16), BF16), shape((nc, 3, cells, 128), F32)),
        in_specs=[VM, VM, SM],
        out_specs=(VM, VM, VM),
        scratch_shapes=scratch,
        compiler_params=PARAMS,
        cost_estimate=cost(nc),
    )(packet, other, weights)
    def call(kernel, outs, extra, offset, up, down, acc, **kw):
        return pl.pallas_call(
            lambda *refs: kernel(offset, *refs),
            out_shape=outs,
            in_specs=[VM, VM, SM, VM, VM, VM],
            out_specs=jax.tree.map(lambda _: VM, outs),
            scratch_shapes=extra + scratch,
            compiler_params=PARAMS,
            cost_estimate=cost(up.shape[0] + down.shape[0]),
            **kw,
        )(up, down, weights, left, tangents, acc)

    def send_on(s, up, down):
        if s == steps:
            up, down = up[: nc // 2], down[nc // 2 :]
        return lax.ppermute(up, "row", forward), lax.ppermute(down, "row", backward)

    up, down = send_on(1, packet, packet)
    offset = nc
    for s in range(1, steps):
        up, down, acc = lax.optimization_barrier((up, down, acc))
        coming = send_on(s + 1, up, down)
        acc = call(step_kernel, acc_shape, [], offset, up, down, acc, input_output_aliases={5: 0})
        offset += 2 * nc
        up, down = coming
    part = shape((nc, COLS, half), F32)
    keep, send = call(last_kernel, (part, part), [pltpu.VMEM(acc_shape.shape, F32)], offset, up, down, acc)
    return keep + lax.ppermute(send, "col", [(0, 1), (1, 0)])


def solution(mesh):
    placed = (P(("grp", "row"), None, "col"), P(("grp", "row"), None, "col"), P("grp"), P("grp"))
    return jax.shard_map(
        body, mesh=mesh, in_specs=placed, out_specs=P(("grp", "row"), None, "col"), check_vma=False
    )
```

```python
import jax
import jax.numpy as jnp
import numpy as np
from jax import lax
from jax.experimental import pallas as pl
from jax.experimental.pallas import tpu as pltpu
from jax.sharding import PartitionSpec as P

F32 = jnp.float32
BF16 = jnp.bfloat16
NN = (((1,), (0,)), ((), ()))
NT = (((1,), (1,)), ((), ()))
COLS = 64
PACK = 80
VM = pl.BlockSpec(memory_space=pltpu.VMEM)
SM = pl.BlockSpec(memory_space=pltpu.SMEM)
PARAMS = pltpu.CompilerParams(vmem_limit_bytes=44 * 2**20)


def squares(g):
    s = g[0:1] * g[0:1] + g[1:2] * g[1:2] + g[2:3] * g[2:3] + g[6:7] * g[6:7]
    s0 = s.astype(BF16).astype(F32)
    s1 = (s - s0).astype(BF16).astype(F32)
    return [s0, s1, s - s0 - s1]


def tiles(sources, weights, offset, left, tangents, acc, d0, d1, k0, k1):
    dist, kern = (d0, d1), (k0, k1)
    nc, half = left.shape[0], d0.shape[1]
    for j, source in enumerate(sources):
        nd = source.shape[0]

        def one(d, carry, source=source, base=offset + sum(s.shape[0] for s in sources[:j])):
            along = source[d, COLS:PACK].astype(F32)
            one_row = jnp.ones_like(along[0:1])
            rows = jnp.concatenate([along[0:3]] + [one_row] * 3 + squares(along) + [jnp.zeros((7, half), F32)], 0)
            rows = rows.astype(BF16)
            for c in range(nc):
                dist[c][...] = lax.dot_general(left[c], rows, NN, preferred_element_type=F32)
            for c in range(nc):
                coupling = 0.0
                for k in range(3):
                    coupling = coupling + jnp.concatenate([tangents[c, k]] * (half // 128), 1) * along[3 + k : 4 + k]
                kern[c][...] = (coupling * lax.rsqrt(dist[c][...])).astype(BF16)
            for c in range(nc):
                part = lax.dot_general(kern[c][...], source[d, 0:COLS], NT, preferred_element_type=F32)
                acc[c] += weights[c, base + d] * part
            return carry

        lax.fori_loop(0, nd, one, 0)


def first_kernel(packet, other, weights, acc, left, tangents, d0, d1, k0, k1):
    half = other.shape[2]
    for c in range(left.shape[0]):
        for h, rows in enumerate((packet[c, COLS:PACK], other[c])):
            g = rows.astype(F32)
            cells = slice(h * half, (h + 1) * half)
            one_row = jnp.ones_like(g[0:1])
            side = jnp.concatenate([-2.0 * g[0:3]] + squares(g) + [one_row] * 3 + [jnp.zeros((7, half), F32)], 0)
            left[c, cells] = side.T.astype(BF16)
            across = jnp.concatenate([g[3:6], jnp.zeros((5, half), F32)], 0).T
            for k in range(3):
                tangents[c, k, cells] = jnp.broadcast_to(across[:, k : k + 1], (half, 128))
    acc[...] = jnp.zeros_like(acc)
    tiles((packet,), weights, 0, left, tangents, acc, d0, d1, k0, k1)


def step_kernel(offset, up, down, weights, left, tangents, acc_in, acc, d0, d1, k0, k1):
    acc[...] = acc_in[...]
    tiles((up, down), weights, offset, left, tangents, acc, d0, d1, k0, k1)


def last_kernel(offset, up, down, weights, left, tangents, acc_in, keep, send, acc, d0, d1, k0, k1):
    acc[...] = acc_in[...]
    tiles((up, down), weights, offset, left, tangents, acc, d0, d1, k0, k1)
    half = keep.shape[2]
    for c in range(keep.shape[0]):
        keep[c] = acc[c, 0:half].T
        send[c] = acc[c, half:].T


def ring_of(n):
    if n == 8:
        return [0, 2, 4, 6, 7, 5, 3, 1]
    return list(range(n))


def body(geometry, currents, pair_count, pair_target):
    nc, _, half = geometry.shape
    n = lax.axis_size("row")
    clusters = pair_count.shape[0]
    shape = jax.ShapeDtypeStruct
    spare = jnp.zeros((nc, PACK - COLS - geometry.shape[1], half), BF16)
    packet = jnp.concatenate([currents, geometry, spare], 1)
    other = lax.ppermute(packet[:, COLS:PACK], "col", [(0, 1), (1, 0)])

    ring = ring_of(n)
    forward = [(ring[i], ring[(i + 1) % n]) for i in range(n)]
    backward = [(b, a) for a, b in forward]
    steps = n // 2
    row = lax.axis_index("row")
    own = row * nc + jnp.arange(nc)
    turn = jnp.arange(n * nc) // nc
    shift = jnp.where(turn % 2 == 1, -((turn + 1) // 2), turn // 2)
    if n == 8:
        spot = (jnp.where(row % 2 == 0, row // 2, n - 1 - row // 2) + shift + n) % n
        chip = jnp.where(spot < n // 2, 2 * spot, 2 * (n - 1 - spot) + 1)
    else:
        chip = (row + shift + n) % n
    second = chip * nc + jnp.arange(n * nc) % nc
    ends = jnp.sum(jnp.where(np.tri(clusters, dtype=bool), pair_count[None, :], 0), 1)
    first_of = jnp.sum((ends[:, None] <= jnp.arange(pair_target.shape[0])[None, :]).astype(jnp.int32), 0)
    is_a = (first_of[None, None, :] == own[:, None, None]) & (pair_target[None, None, :] == second[None, :, None])
    is_b = (first_of[None, None, :] == second[None, :, None]) & (pair_target[None, None, :] == own[:, None, None])
    weights = jnp.sum(is_a.astype(F32) + is_b.astype(F32), 2)

    cells = 2 * half

    def cost(nd):
        count = nc * nd * cells * half
        return pl.CostEstimate(flops=600 * count, bytes_accessed=1 << 20, transcendentals=count)

    scratch = [pltpu.VMEM((cells, half), F32)] * 2 + [pltpu.VMEM((cells, half), BF16)] * 2
    acc_shape = shape((nc, cells, COLS), F32)
    acc, left, tangents = pl.pallas_call(
        first_kernel,
        out_shape=(acc_shape, shape((nc, cells, 16), BF16), shape((nc, 3, cells, 128), F32)),
        in_specs=[VM, VM, SM],
        out_specs=(VM, VM, VM),
        scratch_shapes=scratch,
        compiler_params=PARAMS,
        cost_estimate=cost(nc),
    )(packet, other, weights)
    def call(kernel, outs, extra, offset, up, down, acc, **kw):
        return pl.pallas_call(
            lambda *refs: kernel(offset, *refs),
            out_shape=outs,
            in_specs=[VM, VM, SM, VM, VM, VM],
            out_specs=jax.tree.map(lambda _: VM, outs),
            scratch_shapes=extra + scratch,
            compiler_params=PARAMS,
            cost_estimate=cost(up.shape[0] + down.shape[0]),
            **kw,
        )(up, down, weights, left, tangents, acc)

    def send_on(s, up, down):
        if s == steps:
            up, down = up[: nc // 2], down[nc // 2 :]
        return lax.ppermute(up, "row", forward), lax.ppermute(down, "row", backward)

    up, down = send_on(1, packet, packet)
    offset = nc
    for s in range(1, steps):
        up, down, acc = lax.optimization_barrier((up, down, acc))
        coming = send_on(s + 1, up, down)
        acc = call(step_kernel, acc_shape, [], offset, up, down, acc, input_output_aliases={5: 0})
        offset += 2 * nc
        up, down = coming
    part = shape((nc, COLS, half), F32)
    keep, send = call(last_kernel, (part, part), [pltpu.VMEM(acc_shape.shape, F32)], offset, up, down, acc)
    return keep + lax.ppermute(send, "col", [(0, 1), (1, 0)])


def solution(mesh):
    placed = (P(("grp", "row"), None, "col"), P(("grp", "row"), None, "col"), P("grp"), P("grp"))
    return jax.shard_map(
        body, mesh=mesh, in_specs=placed, out_specs=P(("grp", "row"), None, "col"), check_vma=False
    )
```

```python
import jax
import jax.numpy as jnp
import numpy as np
from jax import lax
from jax.experimental import pallas as pl
from jax.experimental.pallas import tpu as pltpu
from jax.sharding import PartitionSpec as P

F32 = jnp.float32
BF16 = jnp.bfloat16
NN = (((1,), (0,)), ((), ()))
NT = (((1,), (1,)), ((), ()))
COLS = 64
PACK = 80
VM = pl.BlockSpec(memory_space=pltpu.VMEM)
PARAMS = pltpu.CompilerParams(vmem_limit_bytes=44 * 2**20)


def squares(g):
    s = g[0:1] * g[0:1] + g[1:2] * g[1:2] + g[2:3] * g[2:3] + g[6:7] * g[6:7]
    s0 = s.astype(BF16).astype(F32)
    s1 = (s - s0).astype(BF16).astype(F32)
    return [s0, s1, s - s0 - s1]


def tiles(sources, weights, offset, left, tangents, acc, d0, d1, k0, k1):
    dist, kern = (d0, d1), (k0, k1)
    nc, half = left.shape[0], d0.shape[1]
    for j, source in enumerate(sources):
        nd = source.shape[0]

        def one(d, carry, source=source, base=offset + sum(s.shape[0] for s in sources[:j])):
            along = source[d, COLS:PACK].astype(F32)
            one_row = jnp.ones_like(along[0:1])
            rows = jnp.concatenate([along[0:3]] + [one_row] * 3 + squares(along) + [jnp.zeros((7, half), F32)], 0)
            rows = rows.astype(BF16)
            for c in range(nc):
                dist[c][...] = lax.dot_general(left[c], rows, NN, preferred_element_type=F32)
            for c in range(nc):
                coupling = 0.0
                for k in range(3):
                    coupling = coupling + jnp.concatenate([tangents[c, k]] * (half // 128), 1) * along[3 + k : 4 + k]
                kern[c][...] = (coupling * lax.rsqrt(dist[c][...])).astype(BF16)
            for c in range(nc):
                part = lax.dot_general(kern[c][...], source[d, 0:COLS], NT, preferred_element_type=F32)
                acc[c] += weights[c, pl.ds(base + d, 1)] * part
            return carry

        lax.fori_loop(0, nd, one, 0)


def first_kernel(packet, other, weights, acc, left, tangents, d0, d1, k0, k1):
    half = other.shape[2]
    for c in range(left.shape[0]):
        for h, rows in enumerate((packet[c, COLS:PACK], other[c])):
            g = rows.astype(F32)
            cells = slice(h * half, (h + 1) * half)
            one_row = jnp.ones_like(g[0:1])
            side = jnp.concatenate([-2.0 * g[0:3]] + squares(g) + [one_row] * 3 + [jnp.zeros((7, half), F32)], 0)
            left[c, cells] = side.T.astype(BF16)
            across = jnp.concatenate([g[3:6], jnp.zeros((5, half), F32)], 0).T
            for k in range(3):
                tangents[c, k, cells] = jnp.broadcast_to(across[:, k : k + 1], (half, 128))
    acc[...] = jnp.zeros_like(acc)
    tiles((packet,), weights, 0, left, tangents, acc, d0, d1, k0, k1)


def step_kernel(offset, up, down, weights, left, tangents, acc_in, acc, d0, d1, k0, k1):
    acc[...] = acc_in[...]
    tiles((up, down), weights, offset, left, tangents, acc, d0, d1, k0, k1)


def last_kernel(offset, up, down, weights, left, tangents, acc_in, keep, send, acc, d0, d1, k0, k1):
    acc[...] = acc_in[...]
    tiles((up, down), weights, offset, left, tangents, acc, d0, d1, k0, k1)
    half = keep.shape[2]
    for c in range(keep.shape[0]):
        keep[c] = acc[c, 0:half].T
        send[c] = acc[c, half:].T


def ring_of(n):
    if n == 8:
        return [0, 2, 4, 6, 7, 5, 3, 1]
    return list(range(n))


def body(geometry, currents, pair_count, pair_target):
    nc, _, half = geometry.shape
    n = lax.axis_size("row")
    clusters = pair_count.shape[0]
    shape = jax.ShapeDtypeStruct
    spare = jnp.zeros((nc, PACK - COLS - geometry.shape[1], half), BF16)
    packet = jnp.concatenate([currents, geometry, spare], 1)
    other = lax.ppermute(packet[:, COLS:PACK], "col", [(0, 1), (1, 0)])

    ring = ring_of(n)
    forward = [(ring[i], ring[(i + 1) % n]) for i in range(n)]
    backward = [(b, a) for a, b in forward]
    steps = n // 2
    row = lax.axis_index("row")
    own = row * nc + jnp.arange(nc)
    turn = jnp.arange(n * nc) // nc
    shift = jnp.where(turn % 2 == 1, -((turn + 1) // 2), turn // 2)
    if n == 8:
        spot = (jnp.where(row % 2 == 0, row // 2, n - 1 - row // 2) + shift + n) % n
        chip = jnp.where(spot < n // 2, 2 * spot, 2 * (n - 1 - spot) + 1)
    else:
        chip = (row + shift + n) % n
    second = chip * nc + jnp.arange(n * nc) % nc
    ends = jnp.sum(jnp.where(np.tri(clusters, dtype=bool), pair_count[None, :], 0), 1)
    first_of = jnp.sum((ends[:, None] <= jnp.arange(pair_target.shape[0])[None, :]).astype(jnp.int32), 0)
    listed = first_of * clusters + pair_target
    turned = pair_target * clusters + first_of
    wanted = (own[:, None] * clusters + second[None, :])[:, :, None]
    times = jnp.sum((listed == wanted).astype(F32) + (turned == wanted).astype(F32), 2)
    weights = jnp.broadcast_to(times[:, :, None], (nc, n * nc, COLS))

    cells = 2 * half

    def cost(nd):
        count = nc * nd * cells * half
        return pl.CostEstimate(flops=600 * count, bytes_accessed=1 << 20, transcendentals=count)

    scratch = [pltpu.VMEM((cells, half), F32)] * 2 + [pltpu.VMEM((cells, half), BF16)] * 2
    acc_shape = shape((nc, cells, COLS), F32)
    acc, left, tangents = pl.pallas_call(
        first_kernel,
        out_shape=(acc_shape, shape((nc, cells, 16), BF16), shape((nc, 3, cells, 128), F32)),
        in_specs=[VM, VM, VM],
        out_specs=(VM, VM, VM),
        scratch_shapes=scratch,
        compiler_params=PARAMS,
        cost_estimate=cost(nc),
    )(packet, other, weights)
    def call(kernel, outs, extra, offset, up, down, acc, **kw):
        return pl.pallas_call(
            lambda *refs: kernel(offset, *refs),
            out_shape=outs,
            in_specs=[VM] * 6,
            out_specs=jax.tree.map(lambda _: VM, outs),
            scratch_shapes=extra + scratch,
            compiler_params=PARAMS,
            cost_estimate=cost(up.shape[0] + down.shape[0]),
            **kw,
        )(up, down, weights, left, tangents, acc)

    def send_on(s, up, down):
        if s == steps:
            up, down = up[: nc // 2], down[nc // 2 :]
        return lax.ppermute(up, "row", forward), lax.ppermute(down, "row", backward)

    up, down = send_on(1, packet, packet)
    offset = nc
    for s in range(1, steps):
        up, down, acc = lax.optimization_barrier((up, down, acc))
        coming = send_on(s + 1, up, down)
        acc = call(step_kernel, acc_shape, [], offset, up, down, acc, input_output_aliases={5: 0})
        offset += 2 * nc
        up, down = coming
    part = shape((nc, COLS, half), F32)
    keep, send = call(last_kernel, (part, part), [pltpu.VMEM(acc_shape.shape, F32)], offset, up, down, acc)
    return keep + lax.ppermute(send, "col", [(0, 1), (1, 0)])


def solution(mesh):
    placed = (P(("grp", "row"), None, "col"), P(("grp", "row"), None, "col"), P("grp"), P("grp"))
    return jax.shard_map(
        body, mesh=mesh, in_specs=placed, out_specs=P(("grp", "row"), None, "col"), check_vma=False
    )
```

```python
from functools import partial

import jax
import jax.numpy as jnp
import numpy as np
from jax import lax
from jax.experimental import pallas as pl
from jax.experimental.pallas import tpu as pltpu
from jax.sharding import PartitionSpec as P

F32 = jnp.float32
BF16 = jnp.bfloat16
NN = (((1,), (0,)), ((), ()))
NT = (((1,), (1,)), ((), ()))
COLS = 64
PACK = 72
VM = pl.BlockSpec(memory_space=pltpu.VMEM)
PARAMS = pltpu.CompilerParams(vmem_limit_bytes=44 * 2**20)


def squares(g):
    s = g[0:1] * g[0:1] + g[1:2] * g[1:2] + g[2:3] * g[2:3] + g[6:7] * g[6:7]
    s0 = s.astype(BF16).astype(F32)
    s1 = (s - s0).astype(BF16).astype(F32)
    return [s0, s1, s - s0 - s1]


def tiles(sources, weights, offset, left, tangents, acc, d0, d1, k0, k1, start=0):
    dist, kern = (d0, d1), (k0, k1)
    nc, half = left.shape[0], d0.shape[1]
    cells = slice(start, start + d0.shape[0])
    for j, source in enumerate(sources):
        nd = source.shape[0]

        def one(d, carry, source=source, base=offset + sum(s.shape[0] for s in sources[:j])):
            along = source[d][COLS:PACK].astype(F32)
            one_row = jnp.ones_like(along[0:1])
            rows = jnp.concatenate([along[0:3]] + [one_row] * 3 + squares(along) + [jnp.zeros((7, half), F32)], 0)
            rows = rows.astype(BF16)
            for c in range(nc):
                dist[c][...] = lax.dot_general(left[c, cells], rows, NN, preferred_element_type=F32)
            for c in range(nc):
                coupling = 0.0
                for k in range(3):
                    coupling = coupling + jnp.concatenate([tangents[c, k, cells]] * (half // 128), 1) * along[3 + k : 4 + k]
                kern[c][...] = (coupling * lax.rsqrt(dist[c][...])).astype(BF16)
            for c in range(nc):
                part = lax.dot_general(kern[c][...], source[d, 0:COLS], NT, preferred_element_type=F32)
                acc[c] += weights[c, pl.ds(base + d, 1)] * part
            return carry

        lax.fori_loop(0, nd, one, 0)


def first_kernel(packet, other, weights, acc, left, tangents, d0, d1, k0, k1):
    half = other.shape[2]
    for c in range(left.shape[0]):
        for h, rows in enumerate((packet[c][COLS:PACK], other[c])):
            g = rows.astype(F32)
            cells = slice(h * half, (h + 1) * half)
            one_row = jnp.ones_like(g[0:1])
            side = jnp.concatenate([-2.0 * g[0:3]] + squares(g) + [one_row] * 3 + [jnp.zeros((7, half), F32)], 0)
            left[c, cells] = side.T.astype(BF16)
            across = jnp.concatenate([g[3:6], jnp.zeros((5, half), F32)], 0).T
            for k in range(3):
                tangents[c, k, cells] = jnp.broadcast_to(across[:, k : k + 1], (half, 128))
    acc[...] = jnp.zeros_like(acc)
    tiles((packet,), weights, 0, left, tangents, acc, d0, d1, k0, k1)


def step_kernel(offset, up, down, weights, left, tangents, acc_in, acc, d0, d1, k0, k1):
    acc[...] = acc_in[...]
    tiles((up, down), weights, offset, left, tangents, acc, d0, d1, k0, k1)


def last_kernel(offset, start, up, down, weights, left, tangents, acc_in, out, acc, d0, d1, k0, k1):
    half = out.shape[2]
    acc[...] = acc_in[:, start : start + half]
    tiles((up, down), weights, offset, left, tangents, acc, d0, d1, k0, k1, start)
    for c in range(out.shape[0]):
        out[c] = acc[c].T


def ring_of(n):
    if n == 8:
        return [0, 2, 4, 6, 7, 5, 3, 1]
    return list(range(n))


def body(geometry, currents, pair_count, pair_target):
    nc, _, half = geometry.shape
    n = lax.axis_size("row")
    clusters = pair_count.shape[0]
    shape = jax.ShapeDtypeStruct
    spare = jnp.zeros((nc, PACK - COLS - geometry.shape[1], half), BF16)
    packet = jnp.concatenate([currents, geometry, spare], 1)
    other = lax.ppermute(packet[:, COLS:PACK], "col", [(0, 1), (1, 0)])

    ring = ring_of(n)
    forward = [(ring[i], ring[(i + 1) % n]) for i in range(n)]
    backward = [(b, a) for a, b in forward]
    steps = n // 2
    row = lax.axis_index("row")
    own = row * nc + jnp.arange(nc)
    turn = jnp.arange(n * nc) // nc
    shift = jnp.where(turn % 2 == 1, -((turn + 1) // 2), turn // 2)
    if n == 8:
        spot = (jnp.where(row % 2 == 0, row // 2, n - 1 - row // 2) + shift + n) % n
        chip = jnp.where(spot < n // 2, 2 * spot, 2 * (n - 1 - spot) + 1)
    else:
        chip = (row + shift + n) % n
    second = chip * nc + jnp.arange(n * nc) % nc
    ends = jnp.sum(jnp.where(np.tri(clusters, dtype=bool), pair_count[None, :], 0), 1)
    first_of = jnp.sum((ends[:, None] <= jnp.arange(pair_target.shape[0])[None, :]).astype(jnp.int32), 0)
    listed = first_of * clusters + pair_target
    turned = pair_target * clusters + first_of
    wanted = (own[:, None] * clusters + second[None, :])[:, :, None]
    times = jnp.sum((listed == wanted).astype(F32) + (turned == wanted).astype(F32), 2)
    weights = jnp.broadcast_to(times[:, :, None], (nc, n * nc, COLS))

    cells = 2 * half

    def cost(nd):
        count = nc * nd * cells * half
        return pl.CostEstimate(flops=600 * count, bytes_accessed=1 << 20, transcendentals=count)

    scratch = [pltpu.VMEM((cells, half), F32)] * 2 + [pltpu.VMEM((cells, half), BF16)] * 2
    acc_shape = shape((nc, cells, COLS), F32)
    acc, left, tangents = pl.pallas_call(
        first_kernel,
        out_shape=(acc_shape, shape((nc, cells, 16), BF16), shape((nc, 3, cells, 128), F32)),
        in_specs=[VM, VM, VM],
        out_specs=(VM, VM, VM),
        scratch_shapes=scratch,
        compiler_params=PARAMS,
        cost_estimate=cost(nc),
    )(packet, other, weights)
    def call(kernel, outs, scratch, up, down, acc, **kw):
        return pl.pallas_call(
            kernel,
            out_shape=outs,
            in_specs=[VM] * 6,
            out_specs=VM,
            scratch_shapes=scratch,
            compiler_params=PARAMS,
            cost_estimate=cost(up.shape[0] + down.shape[0]),
            **kw,
        )(up, down, weights, left, tangents, acc)

    def send_on(s, up, down):
        if s == steps:
            up, down = up[: nc // 2], down[nc // 2 :]
        return lax.ppermute(up, "row", forward), lax.ppermute(down, "row", backward)

    up, down = send_on(1, packet, packet)
    offset = nc
    for s in range(1, steps):
        up, down, acc = lax.optimization_barrier((up, down, acc))
        coming = send_on(s + 1, up, down)
        acc = call(partial(step_kernel, offset), acc_shape, scratch, up, down, acc, input_output_aliases={5: 0})
        offset += 2 * nc
        up, down = coming
    part = shape((nc, COLS, half), F32)
    small = [pltpu.VMEM((nc, half, COLS), F32)]
    small += [pltpu.VMEM((half, half), F32)] * 2 + [pltpu.VMEM((half, half), BF16)] * 2
    send = call(partial(last_kernel, offset, half), part, small, up, down, acc)
    received = lax.ppermute(send, "col", [(0, 1), (1, 0)])
    keep = call(partial(last_kernel, offset, 0), part, small, up, down, acc)
    return keep + received


def solution(mesh):
    placed = (P(("grp", "row"), None, "col"), P(("grp", "row"), None, "col"), P("grp"), P("grp"))
    return jax.shard_map(
        body, mesh=mesh, in_specs=placed, out_specs=P(("grp", "row"), None, "col"), check_vma=False
    )
```

```python
from functools import partial

import jax
import jax.numpy as jnp
from jax import lax
from jax.experimental import pallas as pl
from jax.experimental.pallas import tpu as pltpu
from jax.sharding import PartitionSpec as P

F32 = jnp.float32
BF16 = jnp.bfloat16
NN = (((1,), (0,)), ((), ()))
NT = (((1,), (1,)), ((), ()))
COLS = 64
PACK = 72
VM = pl.BlockSpec(memory_space=pltpu.VMEM)
PARAMS = pltpu.CompilerParams(vmem_limit_bytes=44 * 2**20)


def squares(g):
    s = g[0:1] * g[0:1] + g[1:2] * g[1:2] + g[2:3] * g[2:3] + g[6:7] * g[6:7]
    s0 = s.astype(BF16).astype(F32)
    s1 = (s - s0).astype(BF16).astype(F32)
    return [s0, s1, s - s0 - s1]


def tiles(sources, weights, offset, left, tangents, acc, d0, d1, k0, k1, start=0):
    dist, kern = (d0, d1), (k0, k1)
    nc, half = left.shape[0], d0.shape[1]
    cells = slice(start, start + d0.shape[0])
    for j, source in enumerate(sources):
        nd = source.shape[0]

        def one(d, carry, source=source, base=offset + sum(s.shape[0] for s in sources[:j])):
            along = source[d][COLS:PACK].astype(F32)
            one_row = jnp.ones_like(along[0:1])
            rows = jnp.concatenate([along[0:3]] + [one_row] * 3 + squares(along) + [jnp.zeros((7, half), F32)], 0)
            rows = rows.astype(BF16)
            for c in range(nc):
                dist[c][...] = lax.dot_general(left[c, cells], rows, NN, preferred_element_type=F32)
            for c in range(nc):
                coupling = 0.0
                for k in range(3):
                    coupling = coupling + jnp.concatenate([tangents[c, k, cells]] * (half // 128), 1) * along[3 + k : 4 + k]
                kern[c][...] = (coupling * lax.rsqrt(dist[c][...])).astype(BF16)
            for c in range(nc):
                part = lax.dot_general(kern[c][...], source[d, 0:COLS], NT, preferred_element_type=F32)
                acc[c] += weights[c, pl.ds(base + d, 1)] * part
            return carry

        lax.fori_loop(0, nd, one, 0)


def first_kernel(packet, other, weights, acc, left, tangents, d0, d1, k0, k1):
    half = other.shape[2]
    for c in range(left.shape[0]):
        for h, rows in enumerate((packet[c][COLS:PACK], other[c])):
            g = rows.astype(F32)
            cells = slice(h * half, (h + 1) * half)
            one_row = jnp.ones_like(g[0:1])
            side = jnp.concatenate([-2.0 * g[0:3]] + squares(g) + [one_row] * 3 + [jnp.zeros((7, half), F32)], 0)
            left[c, cells] = side.T.astype(BF16)
            across = jnp.concatenate([g[3:6], jnp.zeros((5, half), F32)], 0).T
            for k in range(3):
                tangents[c, k, cells] = jnp.broadcast_to(across[:, k : k + 1], (half, 128))
    acc[...] = jnp.zeros_like(acc)
    tiles((packet,), weights, 0, left, tangents, acc, d0, d1, k0, k1)


def step_kernel(offset, up, down, weights, left, tangents, acc_in, acc, d0, d1, k0, k1):
    acc[...] = acc_in[...]
    tiles((up, down), weights, offset, left, tangents, acc, d0, d1, k0, k1)


def last_kernel(offset, start, up, down, weights, left, tangents, acc_in, out, acc, d0, d1, k0, k1):
    half = out.shape[2]
    acc[...] = acc_in[:, start : start + half]
    tiles((up, down), weights, offset, left, tangents, acc, d0, d1, k0, k1, start)
    for c in range(out.shape[0]):
        out[c] = acc[c].T


def ring_of(n):
    if n == 8:
        return [0, 2, 4, 6, 7, 5, 3, 1]
    return list(range(n))


def body(geometry, currents, pair_count, pair_target):
    nc, _, half = geometry.shape
    n = lax.axis_size("row")
    clusters = pair_count.shape[0]
    shape = jax.ShapeDtypeStruct
    spare = jnp.zeros((nc, PACK - COLS - geometry.shape[1], half), BF16)
    packet = jnp.concatenate([currents, geometry, spare], 1)
    other = lax.ppermute(packet[:, COLS:PACK], "col", [(0, 1), (1, 0)])

    ring = ring_of(n)
    forward = [(ring[i], ring[(i + 1) % n]) for i in range(n)]
    backward = [(b, a) for a, b in forward]
    steps = n // 2
    row = lax.axis_index("row")
    own = row * nc + jnp.arange(nc)
    turn = jnp.arange(n * nc) // nc
    shift = jnp.where(turn % 2 == 1, -((turn + 1) // 2), turn // 2)
    if n == 8:
        spot = (jnp.where(row % 2 == 0, row // 2, n - 1 - row // 2) + shift + n) % n
        chip = jnp.where(spot < n // 2, 2 * spot, 2 * (n - 1 - spot) + 1)
    else:
        chip = (row + shift + n) % n
    second = chip * nc + jnp.arange(n * nc) % nc
    lists = lax.optimization_barrier(jnp.concatenate([pair_count, pair_target]))
    pair_count, pair_target = lists[:clusters], lists[clusters:]
    upto = jnp.arange(clusters)[:, None] >= jnp.arange(clusters)[None, :]
    ends = jnp.sum(jnp.where(upto, pair_count[None, :], 0), 1)
    first_of = jnp.sum((ends[:, None] <= jnp.arange(pair_target.shape[0])[None, :]).astype(jnp.int32), 0)
    listed = first_of * clusters + pair_target
    turned = pair_target * clusters + first_of
    wanted = (own[:, None] * clusters + second[None, :])[:, :, None]
    times = jnp.sum((listed == wanted).astype(F32) + (turned == wanted).astype(F32), 2)
    weights = jnp.broadcast_to(times[:, :, None], (nc, n * nc, COLS))

    cells = 2 * half

    def cost(nd):
        count = nc * nd * cells * half
        return pl.CostEstimate(flops=600 * count, bytes_accessed=1 << 20, transcendentals=count)

    scratch = [pltpu.VMEM((cells, half), F32)] * 2 + [pltpu.VMEM((cells, half), BF16)] * 2
    acc_shape = shape((nc, cells, COLS), F32)
    acc, left, tangents = pl.pallas_call(
        first_kernel,
        out_shape=(acc_shape, shape((nc, cells, 16), BF16), shape((nc, 3, cells, 128), F32)),
        in_specs=[VM, VM, VM],
        out_specs=(VM, VM, VM),
        scratch_shapes=scratch,
        compiler_params=PARAMS,
        cost_estimate=cost(nc),
    )(packet, other, weights)
    def call(kernel, outs, scratch, up, down, acc, **kw):
        return pl.pallas_call(
            kernel,
            out_shape=outs,
            in_specs=[VM] * 6,
            out_specs=VM,
            scratch_shapes=scratch,
            compiler_params=PARAMS,
            cost_estimate=cost(up.shape[0] + down.shape[0]),
            **kw,
        )(up, down, weights, left, tangents, acc)

    def send_on(s, up, down):
        if s == steps:
            up, down = up[: nc // 2], down[nc // 2 :]
        return lax.ppermute(up, "row", forward), lax.ppermute(down, "row", backward)

    up, down = send_on(1, packet, packet)
    offset = nc
    for s in range(1, steps):
        up, down, acc = lax.optimization_barrier((up, down, acc))
        coming = send_on(s + 1, up, down)
        acc = call(partial(step_kernel, offset), acc_shape, scratch, up, down, acc, input_output_aliases={5: 0})
        offset += 2 * nc
        up, down = coming
    part = shape((nc, COLS, half), F32)
    small = [pltpu.VMEM((nc, half, COLS), F32)]
    small += [pltpu.VMEM((half, half), F32)] * 2 + [pltpu.VMEM((half, half), BF16)] * 2
    send = call(partial(last_kernel, offset, half), part, small, up, down, acc)
    received = lax.ppermute(send, "col", [(0, 1), (1, 0)])
    keep = call(partial(last_kernel, offset, 0), part, small, up, down, acc)
    return keep + received


def solution(mesh):
    placed = (P(("grp", "row"), None, "col"), P(("grp", "row"), None, "col"), P("grp"), P("grp"))
    return jax.shard_map(
        body, mesh=mesh, in_specs=placed, out_specs=P(("grp", "row"), None, "col"), check_vma=False
    )
```

```python
from functools import partial

import jax
import jax.numpy as jnp
from jax import lax
from jax.experimental import pallas as pl
from jax.experimental.pallas import tpu as pltpu
from jax.sharding import PartitionSpec as P

F32 = jnp.float32
BF16 = jnp.bfloat16
NN = (((1,), (0,)), ((), ()))
NT = (((1,), (1,)), ((), ()))
COLS = 64
PACK = 72
VM = pl.BlockSpec(memory_space=pltpu.VMEM)
PARAMS = pltpu.CompilerParams(vmem_limit_bytes=44 * 2**20)


def squares(g):
    s = g[0:1] * g[0:1] + g[1:2] * g[1:2] + g[2:3] * g[2:3] + g[6:7] * g[6:7]
    s0 = s.astype(BF16).astype(F32)
    s1 = (s - s0).astype(BF16).astype(F32)
    return [s0, s1, s - s0 - s1]


def tiles(sources, weights, offset, left, tangents, acc, stage, d0, d1, k0, k1, start=0):
    dist, kern = (d0, d1), (k0, k1)
    nc, half = left.shape[0], d0.shape[1]
    cells = slice(start, start + d0.shape[0])
    if stage is not None:
        whole = [(source, i) for source in sources for i in range(source.shape[0])]
        for at, (source, i) in enumerate(whole):
            stage[at] = source[i]
        sources = (stage,)

    def one(d, carry, source, base):
        along = source[d][COLS:PACK].astype(F32)
        one_row = jnp.ones_like(along[0:1])
        rows = jnp.concatenate([along[0:3]] + [one_row] * 3 + squares(along) + [jnp.zeros((7, half), F32)], 0)
        rows = rows.astype(BF16)
        for c in range(nc):
            dist[c][...] = lax.dot_general(left[c, cells], rows, NN, preferred_element_type=F32)
        for c in range(nc):
            coupling = 0.0
            for k in range(3):
                coupling = coupling + jnp.concatenate([tangents[c, k, cells]] * (half // 128), 1) * along[3 + k : 4 + k]
            kern[c][...] = (coupling * lax.rsqrt(dist[c][...])).astype(BF16)
        for c in range(nc):
            part = lax.dot_general(kern[c][...], source[d, 0:COLS], NT, preferred_element_type=F32)
            acc[c] += weights[c, pl.ds(base + d, 1)] * part
        return carry

    for source in sources:
        lax.fori_loop(0, source.shape[0], partial(one, source=source, base=offset), 0)
        offset += source.shape[0]


def first_kernel(packet, other, weights, acc, left, tangents, d0, d1, k0, k1):
    half = other.shape[2]
    for c in range(left.shape[0]):
        for h, rows in enumerate((packet[c][COLS:PACK], other[c])):
            g = rows.astype(F32)
            cells = slice(h * half, (h + 1) * half)
            one_row = jnp.ones_like(g[0:1])
            side = jnp.concatenate([-2.0 * g[0:3]] + squares(g) + [one_row] * 3 + [jnp.zeros((7, half), F32)], 0)
            left[c, cells] = side.T.astype(BF16)
            across = jnp.concatenate([g[3:6], jnp.zeros((5, half), F32)], 0).T
            for k in range(3):
                tangents[c, k, cells] = jnp.broadcast_to(across[:, k : k + 1], (half, 128))
    acc[...] = jnp.zeros_like(acc)
    tiles((packet,), weights, 0, left, tangents, acc, None, d0, d1, k0, k1)


def step_kernel(offset, up, down, weights, left, tangents, acc_in, acc, stage, d0, d1, k0, k1):
    acc[...] = acc_in[...]
    tiles((up, down), weights, offset, left, tangents, acc, stage, d0, d1, k0, k1)


def last_kernel(offset, start, up, down, weights, left, tangents, acc_in, out, acc, d0, d1, k0, k1):
    half = out.shape[2]
    acc[...] = acc_in[:, start : start + half]
    tiles((up, down), weights, offset, left, tangents, acc, None, d0, d1, k0, k1, start)
    for c in range(out.shape[0]):
        out[c] = acc[c].T


def ring_of(n):
    if n == 8:
        return [0, 2, 4, 6, 7, 5, 3, 1]
    return list(range(n))


def body(geometry, currents, pair_count, pair_target):
    nc, _, half = geometry.shape
    n = lax.axis_size("row")
    clusters = pair_count.shape[0]
    shape = jax.ShapeDtypeStruct
    spare = jnp.zeros((nc, PACK - COLS - geometry.shape[1], half), BF16)
    packet = jnp.concatenate([currents, geometry, spare], 1)
    other = lax.ppermute(packet[:, COLS:PACK], "col", [(0, 1), (1, 0)])

    ring = ring_of(n)
    forward = [(ring[i], ring[(i + 1) % n]) for i in range(n)]
    backward = [(b, a) for a, b in forward]
    steps = n // 2
    row = lax.axis_index("row")
    own = row * nc + jnp.arange(nc)
    turn = jnp.arange(n * nc) // nc
    shift = jnp.where(turn % 2 == 1, -((turn + 1) // 2), turn // 2)
    if n == 8:
        spot = (jnp.where(row % 2 == 0, row // 2, n - 1 - row // 2) + shift + n) % n
        chip = jnp.where(spot < n // 2, 2 * spot, 2 * (n - 1 - spot) + 1)
    else:
        chip = (row + shift + n) % n
    second = chip * nc + jnp.arange(n * nc) % nc
    lists = lax.optimization_barrier(jnp.concatenate([pair_count, pair_target]))
    pair_count, pair_target = lists[:clusters], lists[clusters:]
    upto = jnp.arange(clusters)[:, None] >= jnp.arange(clusters)[None, :]
    ends = jnp.sum(jnp.where(upto, pair_count[None, :], 0), 1)
    first_of = jnp.sum((ends[:, None] <= jnp.arange(pair_target.shape[0])[None, :]).astype(jnp.int32), 0)
    listed = first_of * clusters + pair_target
    turned = pair_target * clusters + first_of
    wanted = (own[:, None] * clusters + second[None, :])[:, :, None]
    times = jnp.sum((listed == wanted).astype(F32) + (turned == wanted).astype(F32), 2)
    weights = jnp.broadcast_to(times[:, :, None], (nc, n * nc, COLS))

    cells = 2 * half

    def cost(nd):
        count = nc * nd * cells * half
        return pl.CostEstimate(flops=600 * count, bytes_accessed=1 << 20, transcendentals=count)

    scratch = [pltpu.VMEM((cells, half), F32)] * 2 + [pltpu.VMEM((cells, half), BF16)] * 2
    acc_shape = shape((nc, cells, COLS), F32)
    acc, left, tangents = pl.pallas_call(
        first_kernel,
        out_shape=(acc_shape, shape((nc, cells, 16), BF16), shape((nc, 3, cells, 128), F32)),
        in_specs=[VM, VM, VM],
        out_specs=(VM, VM, VM),
        scratch_shapes=scratch,
        compiler_params=PARAMS,
        cost_estimate=cost(nc),
    )(packet, other, weights)
    def call(kernel, outs, scratch, up, down, acc, **kw):
        return pl.pallas_call(
            kernel,
            out_shape=outs,
            in_specs=[VM] * 6,
            out_specs=VM,
            scratch_shapes=scratch,
            compiler_params=PARAMS,
            cost_estimate=cost(up.shape[0] + down.shape[0]),
            **kw,
        )(up, down, weights, left, tangents, acc)

    def send_on(s, up, down):
        if s == steps:
            up, down = up[: nc // 2], down[nc // 2 :]
        return lax.ppermute(up, "row", forward), lax.ppermute(down, "row", backward)

    up, down = send_on(1, packet, packet)
    offset = nc
    for s in range(1, steps):
        up, down, acc = lax.optimization_barrier((up, down, acc))
        coming = send_on(s + 1, up, down)
        acc = call(partial(step_kernel, offset), acc_shape, [pltpu.VMEM((2 * nc, PACK, half), BF16)] + scratch, up, down, acc, input_output_aliases={5: 0})
        offset += 2 * nc
        up, down = coming
    part = shape((nc, COLS, half), F32)
    small = [pltpu.VMEM((nc, half, COLS), F32)]
    small += [pltpu.VMEM((half, half), F32)] * 2 + [pltpu.VMEM((half, half), BF16)] * 2
    send = call(partial(last_kernel, offset, half), part, small, up, down, acc)
    received = lax.ppermute(send, "col", [(0, 1), (1, 0)])
    keep = call(partial(last_kernel, offset, 0), part, small, up, down, acc)
    return keep + received


def solution(mesh):
    placed = (P(("grp", "row"), None, "col"), P(("grp", "row"), None, "col"), P("grp"), P("grp"))
    return jax.shard_map(
        body, mesh=mesh, in_specs=placed, out_specs=P(("grp", "row"), None, "col"), check_vma=False
    )
```

```python
from functools import partial

import jax
import jax.numpy as jnp
from jax import lax
from jax.experimental import pallas as pl
from jax.experimental.pallas import tpu as pltpu
from jax.sharding import PartitionSpec as P

F32 = jnp.float32
BF16 = jnp.bfloat16
NN = (((1,), (0,)), ((), ()))
NT = (((1,), (1,)), ((), ()))
COLS = 64
PACK = 72
VM = pl.BlockSpec(memory_space=pltpu.VMEM)
PARAMS = pltpu.CompilerParams(vmem_limit_bytes=44 * 2**20)


def squares(g):
    s = g[0:1] * g[0:1] + g[1:2] * g[1:2] + g[2:3] * g[2:3] + g[6:7] * g[6:7]
    s0 = s.astype(BF16).astype(F32)
    s1 = (s - s0).astype(BF16).astype(F32)
    return [s0, s1, s - s0 - s1]


def tiles(sources, weights, offset, left, tangents, acc, stage, d0, d1, k0, k1, start=0):
    dist, kern = (d0, d1), (k0, k1)
    nc, half = left.shape[0], d0.shape[1]
    cells = slice(start, start + d0.shape[0])
    if stage is not None:
        whole = [(source, i) for source in sources for i in range(source.shape[0])]
        for at, (source, i) in enumerate(whole):
            stage[at] = source[i]
        sources = (stage,)

    def one(d, carry, source, base):
        along = source[d][COLS:PACK].astype(F32)
        one_row = jnp.ones_like(along[0:1])
        rows = jnp.concatenate([along[0:3]] + [one_row] * 3 + squares(along) + [jnp.zeros((7, half), F32)], 0)
        rows = rows.astype(BF16)
        for c in range(nc):
            dist[c][...] = lax.dot_general(left[c, cells], rows, NN, preferred_element_type=F32)
        for c in range(nc):
            coupling = 0.0
            for k in range(3):
                coupling = coupling + jnp.concatenate([tangents[c, k, cells]] * (half // 128), 1) * along[3 + k : 4 + k]
            kern[c][...] = (coupling * lax.rsqrt(dist[c][...])).astype(BF16)
        for c in range(nc):
            part = lax.dot_general(kern[c][...], source[d, 0:COLS], NT, preferred_element_type=F32)
            acc[c] += weights[c, pl.ds(base + d, 1)] * part
        return carry

    for source in sources:
        lax.fori_loop(0, source.shape[0], partial(one, source=source, base=offset), 0)
        offset += source.shape[0]


def first_kernel(packet, other, weights, acc, left, tangents, d0, d1, k0, k1):
    half = other.shape[2]
    for c in range(left.shape[0]):
        for h, rows in enumerate((packet[c][COLS:PACK], other[c])):
            g = rows.astype(F32)
            cells = slice(h * half, (h + 1) * half)
            one_row = jnp.ones_like(g[0:1])
            side = jnp.concatenate([-2.0 * g[0:3]] + squares(g) + [one_row] * 3 + [jnp.zeros((7, half), F32)], 0)
            left[c, cells] = side.T.astype(BF16)
            across = jnp.concatenate([g[3:6], jnp.zeros((5, half), F32)], 0).T
            for k in range(3):
                tangents[c, k, cells] = jnp.broadcast_to(across[:, k : k + 1], (half, 128))
    acc[...] = jnp.zeros_like(acc)
    tiles((packet,), weights, 0, left, tangents, acc, None, d0, d1, k0, k1)


def step_kernel(offset, up, down, weights, left, tangents, acc_in, acc, stage, d0, d1, k0, k1):
    acc[...] = acc_in[...]
    tiles((up, down), weights, offset, left, tangents, acc, stage, d0, d1, k0, k1)


def last_kernel(offset, start, up, down, weights, left, tangents, acc_in, out, acc, d0, d1, k0, k1):
    half = out.shape[2]
    acc[...] = acc_in[:, start : start + half]
    tiles((up, down), weights, offset, left, tangents, acc, None, d0, d1, k0, k1, start)
    for c in range(out.shape[0]):
        out[c] = acc[c].T


def ring_of(n):
    if n == 8:
        return [0, 2, 4, 6, 7, 5, 3, 1]
    return list(range(n))


def body(geometry, currents, pair_count, pair_target):
    nc, _, half = geometry.shape
    n = lax.axis_size("row")
    clusters = pair_count.shape[0]
    shape = jax.ShapeDtypeStruct
    spare = jnp.zeros((nc, PACK - COLS - geometry.shape[1], half), BF16)
    packet = jnp.concatenate([currents, geometry, spare], 1)
    other = lax.ppermute(packet[:, COLS:PACK], "col", [(0, 1), (1, 0)])

    ring = ring_of(n)
    forward = [(ring[i], ring[(i + 1) % n]) for i in range(n)]
    there = [(2 * a, 2 * b) for a, b in forward] + [(2 * b + 1, 2 * a + 1) for a, b in forward]
    back = [(b, a) for a, b in there]
    steps = n // 2
    row = lax.axis_index("row")
    own = row * nc + jnp.arange(nc)
    turn = jnp.arange(n * nc) // nc
    shift = jnp.where(turn % 2 == 1, -((turn + 1) // 2), turn // 2)
    shift = jnp.where(lax.axis_index("col") == 1, -shift, shift)
    if n == 8:
        spot = (jnp.where(row % 2 == 0, row // 2, n - 1 - row // 2) + shift + n) % n
        chip = jnp.where(spot < n // 2, 2 * spot, 2 * (n - 1 - spot) + 1)
    else:
        chip = (row + shift + n) % n
    second = chip * nc + jnp.arange(n * nc) % nc
    lists = lax.optimization_barrier(jnp.concatenate([pair_count, pair_target]))
    pair_count, pair_target = lists[:clusters], lists[clusters:]
    upto = jnp.arange(clusters)[:, None] >= jnp.arange(clusters)[None, :]
    ends = jnp.sum(jnp.where(upto, pair_count[None, :], 0), 1)
    first_of = jnp.sum((ends[:, None] <= jnp.arange(pair_target.shape[0])[None, :]).astype(jnp.int32), 0)
    listed = first_of * clusters + pair_target
    turned = pair_target * clusters + first_of
    wanted = (own[:, None] * clusters + second[None, :])[:, :, None]
    times = jnp.sum((listed == wanted).astype(F32) + (turned == wanted).astype(F32), 2)
    weights = jnp.broadcast_to(times[:, :, None], (nc, n * nc, COLS))

    cells = 2 * half

    def cost(nd):
        count = nc * nd * cells * half
        return pl.CostEstimate(flops=600 * count, bytes_accessed=1 << 20, transcendentals=count)

    scratch = [pltpu.VMEM((cells, half), F32)] * 2 + [pltpu.VMEM((cells, half), BF16)] * 2
    acc_shape = shape((nc, cells, COLS), F32)
    acc, left, tangents = pl.pallas_call(
        first_kernel,
        out_shape=(acc_shape, shape((nc, cells, 16), BF16), shape((nc, 3, cells, 128), F32)),
        in_specs=[VM, VM, VM],
        out_specs=(VM, VM, VM),
        scratch_shapes=scratch,
        compiler_params=PARAMS,
        cost_estimate=cost(nc),
    )(packet, other, weights)
    def call(kernel, outs, scratch, up, down, acc, **kw):
        return pl.pallas_call(
            kernel,
            out_shape=outs,
            in_specs=[VM] * 6,
            out_specs=VM,
            scratch_shapes=scratch,
            compiler_params=PARAMS,
            cost_estimate=cost(up.shape[0] + down.shape[0]),
            **kw,
        )(up, down, weights, left, tangents, acc)

    def send_on(s, up, down):
        if s == steps:
            up, down = up[: nc // 2], down[nc // 2 :]
        return lax.ppermute(up, ("row", "col"), there), lax.ppermute(down, ("row", "col"), back)

    up, down = send_on(1, packet, packet)
    offset = nc
    for s in range(1, steps):
        up, down, acc = lax.optimization_barrier((up, down, acc))
        coming = send_on(s + 1, up, down)
        acc = call(partial(step_kernel, offset), acc_shape, [pltpu.VMEM((2 * nc, PACK, half), BF16)] + scratch, up, down, acc, input_output_aliases={5: 0})
        offset += 2 * nc
        up, down = coming
    part = shape((nc, COLS, half), F32)
    small = [pltpu.VMEM((nc, half, COLS), F32)]
    small += [pltpu.VMEM((half, half), F32)] * 2 + [pltpu.VMEM((half, half), BF16)] * 2
    send = call(partial(last_kernel, offset, half), part, small, up, down, acc)
    received = lax.ppermute(send, "col", [(0, 1), (1, 0)])
    keep = call(partial(last_kernel, offset, 0), part, small, up, down, acc)
    return keep + received


def solution(mesh):
    placed = (P(("grp", "row"), None, "col"), P(("grp", "row"), None, "col"), P("grp"), P("grp"))
    return jax.shard_map(
        body, mesh=mesh, in_specs=placed, out_specs=P(("grp", "row"), None, "col"), check_vma=False
    )
```
